512 devices in a mesh: row: 32 (over y, x), col: 16 (over z, core).
Axes of the slice: x: 4, y: 8, z: 8, core: 2. Of those that a mesh axis runs over, the one named last changes fastest.
Arguments:
- panel: float32 [1048576, 128], P(('row', 'col')), may hold values from -400 to 400
- next_panel: float32 [1048576, 128], P(('row', 'col')), may hold values from -600 to 600
Outputs:
- q_panel: float32 [1048576, 128], P(('row', 'col'))
- r_factor: float32 [128, 128], replicated
- coupling: float32 [128, 128], replicated
- trailing: float32 [1048576, 128], P(('row', 'col'))
The draws below stay inside these ranges and needn't reach their ends.
All inputs are finite; a program needn't handle non-finite values.
Results may differ from the reference program's by a relative error of at most 0.00075.
Values sent between devices are 32-bit elements; how exact they have to be, the bound alone decides.
A program may use at most 64 MiB of HBM per device.

```python
import jax
import jax.numpy as jnp
from jax import lax

PANEL = 128
ROWS = 1048576


def shared_panel(key, nearness):
    keys = jax.random.split(key, 6)
    base = jax.random.normal(keys[0], (ROWS, PANEL), jnp.float32)
    columns = jnp.arange(PANEL, dtype=jnp.int32)
    partner = columns - columns % 2
    odd_mask = (columns % 2).astype(jnp.float32)[None, :]
    mixed = jnp.take(base, partner, axis=1) + nearness * odd_mask * base
    column_order = jax.random.permutation(keys[5], PANEL)
    mixed = jnp.take(mixed, column_order, axis=1)
    place = jnp.arange(ROWS, dtype=jnp.float32)[:, None] / ROWS
    row_scale = 10.0 ** (jax.random.uniform(keys[3], (ROWS, 1), jnp.float32) - 0.5) * 3.0 ** (place - 0.5)
    col_scale = 10.0 ** (jax.random.uniform(keys[4], (1, PANEL), jnp.float32) - 0.5)
    return (mixed * row_scale * col_scale, row_scale)


def draw_panel(key, part):
    values, scales = shared_panel(key, 0.005)
    return values


def draw_next_panel(key, part):
    values, scales = shared_panel(key, 0.005)
    key = jax.random.fold_in(key, 23)
    noise = jax.random.normal(key, (ROWS, PANEL), jnp.float32)
    return 0.8 * values + 0.4 * jnp.roll(values, 1, axis=1) + 0.6 * scales * noise


def setup_inputs(seed: int = 0) -> dict:
    splits = jax.random.split(jax.random.key(seed), 3)
    panel = draw_panel(jax.random.fold_in(splits[2], 71), 0)
    next_panel = draw_next_panel(jax.random.fold_in(splits[2], 71), 0)
    return dict(panel=panel, next_panel=next_panel)


def factor(gram):
    eye = jnp.eye(gram.shape[0], dtype=gram.dtype)
    lower = jnp.linalg.cholesky(gram)
    lower_inv = lax.linalg.triangular_solve(lower, eye, left_side=True, lower=True)
    return (lower.T, lower_inv.T)

def inner(left, right):
    return jnp.einsum('rp,rq->pq', left, right, precision=lax.Precision.HIGHEST)

def times(left, right):
    return jnp.dot(left, right, precision=lax.Precision.HIGHEST)

def reference(panel, next_panel):
    count = panel.shape[0]
    gram_first = inner(panel, panel) / count
    first_r, first_inv = factor(gram_first)
    draft = times(panel, first_inv)
    gram_second = inner(draft, draft) / count
    second_r, second_inv = factor(gram_second)
    q_panel = times(draft, second_inv)
    r_factor = times(second_r, first_r)
    coupling = inner(q_panel, next_panel) / count
    trailing = next_panel - times(q_panel, coupling)
    return (q_panel, r_factor, coupling, trailing)
```

```python
import functools

import jax
import jax.numpy as jnp
from jax import lax
from jax.experimental import pallas as pl
from jax.experimental.pallas import tpu as pltpu
from jax.sharding import PartitionSpec as P

MESH = pl.DeviceIdType.MESH
F32 = jnp.float32
BF16 = jnp.bfloat16
HIGHEST = lax.Precision.HIGHEST
N = 128
T = N // 8
HALF = T // 2
ROW_X = 4
ROW_Y = 8
COL_K = 2
COL_Z = 8
CHUNKS = ROW_X * COL_K
HI, LO, CO, DG, USED, PADDED = 0, 8, 16, 32, 34, 40


def two_sum(a, b):
    s = a + b
    t = s - a
    return s, (a - (s - t)) + (b - t)


def quick_sum(a, b):
    s = a + b
    return s, b - (s - a)


def unit(x):
    q = x * (2.0**23 + 1.0)
    return jnp.abs(q - q * (1.0 - 2.0**-24))


def pieces(x, sigma):
    s1 = (x + sigma) - sigma
    x = x - s1
    sigma = sigma * 2.0**-8
    s2 = (x + sigma) - sigma
    x = x - s2
    sigma = sigma * 2.0**-8
    s3 = (x + sigma) - sigma
    return s1.astype(BF16), s2.astype(BF16), s3.astype(BF16), (x - s3).astype(BF16)


def split3(x):
    a = x.astype(BF16)
    x = x - a.astype(F32)
    b = x.astype(BF16)
    return a, b, (x - b.astype(F32)).astype(BF16)


def tdot(a, b):
    return lax.dot_general(a, b, (((0,), (0,)), ((), ())), preferred_element_type=F32)


def dot(a, b, dims=((1,), (0,))):
    return lax.dot_general(a, b, (dims, ((), ())), precision=HIGHEST, preferred_element_type=F32)


def lane_sub():
    shape = (8, N)
    return lax.broadcasted_iota(jnp.int32, shape, 1), lax.broadcasted_iota(jnp.int32, shape, 0)


def fold(top, low, i):
    lane, sub = lane_sub()
    off = lane - 8 * i
    far = lane - 8 * (T - 1 - i)
    left = pltpu.roll(low, (8 * i + 8) % N, 1)
    block = pltpu.roll(low, (16 * i + 8) % N, 1)
    tile = jnp.where(off > sub, jnp.where(off < 8, block, left), top)
    diag = jnp.sum(jnp.where(far == sub, low, 0.0), axis=0, keepdims=True)
    return tile, diag


def unfold(tile, diag, i):
    lane, sub = lane_sub()
    off = lane - 8 * i
    far = lane - 8 * (T - 1 - i)
    top = jnp.where(off <= sub, tile, 0.0)
    left = pltpu.roll(tile, (N - 8 * i - 8) % N, 1)
    block = pltpu.roll(tile, (N - 16 * i - 8) % N, 1)
    low = jnp.where(far < 0, left, jnp.where(far == sub, diag, 0.0))
    upper = jnp.where((far > sub) & (far < 8), block, 0.0)
    return top, low, upper


def merge(slots):
    n = slots.shape[0]

    def pair(h, l, rows):
        hs, ls = slots[0, pl.ds(h, rows)], slots[0, pl.ds(l, rows)]
        for j in range(1, n):
            hs, e = two_sum(hs, slots[j, pl.ds(h, rows)])
            ls = ls + (slots[j, pl.ds(l, rows)] + e)
        return quick_sum(hs, ls)

    hi, lo = pair(HI, LO, 8)
    dh, dl = pair(DG, DG + 1, 1)
    co = slots[0, pl.ds(CO, 16)]
    for j in range(1, n):
        co = co + slots[j, pl.ds(CO, 16)]
    return hi, lo, co, dh, dl


def put(ref, parts):
    hi, lo, co, dh, dl = parts
    ref[pl.ds(HI, 8)] = hi
    ref[pl.ds(LO, 8)] = lo
    ref[pl.ds(CO, 16)] = co
    ref[pl.ds(DG, 1)] = dh
    ref[pl.ds(DG + 1, 1)] = dl


def sums_kernel(
    panel_hbm, next_hbm, out_ref,
    panel, nxt, ps, ns, first, got1, mine1, got2, mine2, got3, mine3, got4, in_sem, send_sem, recv_sem,
):
    rows = panel.shape[0]
    load_p = pltpu.make_async_copy(panel_hbm, panel, in_sem.at[0])
    load_n = pltpu.make_async_copy(next_hbm, nxt, in_sem.at[1])
    load_p.start()
    load_n.start()
    r, c = lax.axis_index("row"), lax.axis_index("col")
    y, x = lax.div(r, ROW_X), lax.rem(r, ROW_X)
    z, k = lax.div(c, COL_K), lax.rem(c, COL_K)
    g = x * COL_K + k

    def near(i):
        return (y * ROW_X + lax.div(i, COL_K), z * COL_K + lax.rem(i, COL_K))

    def along_z(i):
        return (r, i * COL_K + k)

    def along_y(i):
        return (i * ROW_X + x, c)

    groups = ((CHUNKS, g, near), (COL_Z, z, along_z), (ROW_Y, y, along_y))
    barrier = pltpu.get_barrier_semaphore()
    for n, me, at in groups:
        for j in range(1, n):
            pl.semaphore_signal(barrier, inc=1, device_id=at(lax.rem(me + j, n)), device_id_type=MESH)

    load_p.wait()
    block = 256
    def largest(i, m):
        v = jnp.abs(panel[pl.ds(pl.multiple_of(i * block, block), block), :])
        return jnp.maximum(m, jnp.max(v.reshape(block // 8, 8, N), axis=0))
    m = lax.fori_loop(0, rows // block, largest, jnp.zeros((8, N), F32))
    m = jnp.max(m, axis=0, keepdims=True)
    sigma = unit(m) * (1.5 * 2.0**17)

    def cut_p(i, _):
        at = pl.ds(pl.multiple_of(i * block, block), block)
        for j, s in enumerate(pieces(panel[at, :], sigma)):
            ps[at, pl.ds(j * N, N)] = s
        return 0
    lax.fori_loop(0, rows // block, cut_p, 0)
    load_n.wait()
    def cut_n(i, _):
        at = pl.ds(pl.multiple_of(i * block, block), block)
        for j, s in enumerate(split3(nxt[at, :])):
            ns[at, pl.ds(j * N, N)] = s
        return 0
    lax.fori_loop(0, rows // block, cut_n, 0)

    hi = lo = jnp.zeros((N, N), F32)
    low = cross = jnp.zeros((N, N), F32)
    step = 1024
    for i in range(0, rows, step):
        at = pl.ds(i, step)
        p12, p34 = ps[at, 0:2 * N], ps[at, 2 * N:4 * N]
        e = tdot(p12, p12)
        f = tdot(p12, p34)
        hi, err = two_sum(hi, e[:N, :N])
        lo = lo + err
        hi, err = two_sum(hi, e[:N, N:] + e[N:, :N])
        lo = lo + err + e[N:, N:]
        low = low + ((f[:N, :N] + f[:N, N:]) + (f[N:, :N] + f[N:, N:]))
        n12, n3 = ns[at, 0:2 * N], ns[at, 2 * N:3 * N]
        u = tdot(p12, n12)
        w = tdot(p34, n12)
        v = tdot(p12, n3)
        cross = cross + (u[:N, :N] + ((u[:N, N:] + u[N:, :N]) + (u[N:, N:] + w[:N, :N] + w[:N, N:] + w[N:, :N] + v[:N] + v[N:])))
    lo = lo + (low + low.T)
    hi, lo = quick_sum(hi, lo)
    for i in range(CHUNKS):
        a, b = slice(8 * i, 8 * i + 8), slice(8 * (T - 1 - i), 8 * (T - i))
        ht, hd = fold(hi[a], hi[b], i)
        lt, ld = fold(lo[a], lo[b], i)
        put(first.at[i], (ht, lt, cross[16 * i:16 * i + 16], hd, ld))

    pl.semaphore_wait(barrier, sum(n - 1 for n, _, _ in groups))

    def spread(phase, group, source, target):
        n, me, at = group
        for j in range(1, n):
            to = lax.rem(me + j, n)
            pltpu.make_async_remote_copy(
                source(to).at[pl.ds(0, USED)], target(j).at[pl.ds(0, USED)],
                send_sem.at[phase], recv_sem.at[phase], device_id=at(to), device_id_type=MESH,
            ).start()

    def arrived(sem, phase, n):
        whole = first.at[pl.ds(0, n - 1), pl.ds(0, USED)]
        pltpu.make_async_copy(whole, whole, sem.at[phase]).wait()

    spread(0, groups[0], lambda to: first.at[to], lambda j: got1.at[CHUNKS - j])
    got1[0] = first[g]
    arrived(recv_sem, 0, CHUNKS)
    put(mine1, merge(got1))
    spread(1, groups[1], lambda to: mine1, lambda j: got2.at[z])
    got2[z] = mine1[...]
    arrived(recv_sem, 1, COL_Z)
    put(mine2, merge(got2))
    spread(2, groups[2], lambda to: mine2, lambda j: got3.at[y])
    got3[y] = mine2[...]
    arrived(recv_sem, 2, ROW_Y)
    put(mine3, merge(got3))
    spread(3, groups[0], lambda to: mine3, lambda j: got4.at[g])
    got4[g] = mine3[...]
    arrived(recv_sem, 3, CHUNKS)
    out_ref[...] = got4[...]
    for phase, n in enumerate((CHUNKS, COL_Z, ROW_Y, CHUNKS)):
        arrived(send_sem, phase, n)


def lanes(v, i):
    return jnp.broadcast_to(v[:, i:i + 1], (8, N))


def subs(v, i):
    return jnp.broadcast_to(v[i:i + 1, :], (8, N))


def factor(gram, upper, lower_inv):
    lane, sub = lane_sub()
    a = [gram[8 * b:8 * b + 8, :] for b in range(T)]
    for b in range(T):
        off = lane - 8 * b
        inside = (off >= 0) & (off < 8)
        t = [lanes(a[b], 8 * b + i) for i in range(8)]
        v = jnp.where(inside, jnp.where(off == sub, 1.0, 0.0), a[b])
        g, h = [], {}
        pivots = jnp.ones((8, N), F32)
        for i in range(8):
            d = subs(t[i], i)
            inv = 1.0 / d
            pivots = jnp.where(sub == i, d, pivots)
            g.append(inv * subs(v, i))
            for j in range(i + 1, 8):
                h[i, j] = inv * subs(t[j], i)
            if i < 7:
                below = jnp.where(sub > i, t[i], 0.0)
                v = v - below * g[i]
                for j in range(i + 1, 8):
                    t[j] = t[j] - below * h[i, j]
        scale = lax.rsqrt(pivots)
        lower_inv[8 * b:8 * b + 8, :] = jnp.where(off < 8, v * scale, 0.0)
        u = v
        for j in range(8):
            u = jnp.where(off == j, jnp.where(sub <= j, t[j], 0.0), u)
        upper[8 * b:8 * b + 8, :] = jnp.where(off < 0, 0.0, u * scale)
        for b2 in range(b + 1, T):
            t2 = [lanes(a[b2], 8 * b + i) for i in range(8)]
            v2 = jnp.where(inside, 0.0, a[b2])
            for i in range(8):
                v2 = v2 - t2[i] * g[i]
                for j in range(i + 1, 8):
                    t2[j] = t2[j] - t2[i] * h[i, j]
            a[b2] = v2


def finish_kernel(
    sums, panel_hbm, next_hbm, q_hbm, r_ref, coupling_ref, trailing_hbm,
    panel, nxt, q, trail, hi_ref, lo_ref, gram, r1, x1, gram2, r2, x2, both, in_sem, out_sem, *, count,
):
    rows = panel.shape[0]
    load_p = pltpu.make_async_copy(panel_hbm, panel, in_sem.at[0])
    load_n = pltpu.make_async_copy(next_hbm, nxt, in_sem.at[1])
    load_p.start()
    load_n.start()
    for i in range(HALF):
        a, b = slice(8 * i, 8 * i + 8), slice(8 * (T - 1 - i), 8 * (T - i))
        for ref, at, dg in ((hi_ref, HI, DG), (lo_ref, LO, DG + 1)):
            top, low, up = unfold(sums[i, pl.ds(at, 8)], sums[i, pl.ds(dg, 1)], i)
            ref[0, a, :] = top
            ref[0, b, :] = low
            ref[1, a, :] = jnp.zeros_like(up)
            ref[1, b, :] = up
    row_id = lax.broadcasted_iota(jnp.int32, (N, N), 0)
    col_id = lax.broadcasted_iota(jnp.int32, (N, N), 1)

    def whole(ref):
        low = ref[0]
        up = ref[1]
        mirrored = jnp.where(col_id > row_id, (low + up.T).T, 0.0)
        return jnp.where(col_id > row_id, mirrored, low + up.T)

    hi, lo = whole(hi_ref) / count, whole(lo_ref) / count
    eye = row_id == col_id
    diag = jnp.where(eye, hi, 0.0)
    s_row = unit(lax.rsqrt(jnp.sum(diag, axis=0, keepdims=True)))
    s_col = unit(lax.rsqrt(jnp.sum(diag, axis=1, keepdims=True)))
    hi = hi * s_row * s_col
    lo = lo * s_row * s_col
    gram[...] = hi
    factor(gram, r1, x1)
    s1, s2, s3, s4 = pieces(r1[...], 1.5 * 2.0**15)
    p12, p34 = jnp.concatenate([s1, s2], 1), jnp.concatenate([s3, s4], 1)
    e = tdot(p12, p12)
    f = tdot(p12, p34)
    low = (f[:N, :N] + f[:N, N:]) + (f[N:, :N] + f[N:, N:])
    low = (low + low.T) + e[N:, N:]
    rest, e1 = two_sum(hi, -e[:N, :N])
    rest, e2 = two_sum(rest, -(e[:N, N:] + e[N:, :N]))
    rest = rest + ((e1 + e2) + (lo - low))
    x = x1[...]
    m = dot(x, r1[...], ((1,), (1,)))
    gram2[...] = dot(m, m, ((1,), (1,))) + dot(dot(x, rest), x, ((1,), (1,)))
    factor(gram2, r2, x2)
    r_ref[...] = dot(r2[...], r1[...]) / s_row
    w = dot(x, x2[...], ((0,), (1,))) * s_col
    cross = jnp.concatenate([sums[i, pl.ds(CO, 16)] for i in range(CHUNKS)], 0) / count
    coupling = dot(w, cross, ((0,), (0,)))
    coupling_ref[...] = coupling
    both[:, 0:N] = w
    both[:, N:2 * N] = dot(w, coupling)
    load_p.wait()
    load_n.wait()
    block = 256
    copies = []
    for i in range(0, rows, block):
        at = pl.ds(i, block)
        o = dot(panel[at, :], both[...])
        q[at, :] = o[:, :N]
        trail[at, :] = nxt[at, :] - o[:, N:]
        for src, dst, j in ((q, q_hbm, 0), (trail, trailing_hbm, 1)):
            copy = pltpu.make_async_copy(src.at[at], dst.at[at], out_sem.at[j, i // block])
            copy.start()
            copies.append(copy)
    for copy in copies:
        copy.wait()


def shards(panel, next_panel):
    rows = panel.shape[0]
    count = rows * lax.axis_size("row") * lax.axis_size("col")
    any_, vmem = pl.BlockSpec(memory_space=pl.ANY), pl.BlockSpec(memory_space=pltpu.VMEM)
    small = pltpu.VMEM((N, N), F32)
    tall = pltpu.VMEM((rows, N), F32)
    slots = pltpu.VMEM((CHUNKS, PADDED, N), F32)
    one = pltpu.VMEM((PADDED, N), F32)
    sums = pl.pallas_call(
        sums_kernel,
        name="sums",
        out_shape=jax.ShapeDtypeStruct((CHUNKS, PADDED, N), F32),
        in_specs=[any_, any_],
        out_specs=vmem,
        scratch_shapes=[
            tall, tall, pltpu.VMEM((rows, 4 * N), BF16), pltpu.VMEM((rows, 3 * N), BF16),
            slots, slots, one, slots, one, slots, one, slots,
            pltpu.SemaphoreType.DMA((2,)), pltpu.SemaphoreType.DMA((4,)), pltpu.SemaphoreType.DMA((4,)),
        ],
        compiler_params=pltpu.CompilerParams(collective_id=0, has_side_effects=True, vmem_limit_bytes=32 << 20),
    )(panel, next_panel)
    big = jax.ShapeDtypeStruct((rows, N), F32)
    little = jax.ShapeDtypeStruct((N, N), F32)
    q, r, coupling, trailing = pl.pallas_call(
        functools.partial(finish_kernel, count=count),
        name="finish",
        out_shape=(big, little, little, big),
        in_specs=[vmem, any_, any_],
        out_specs=(any_, vmem, vmem, any_),
        scratch_shapes=[
            tall, tall, tall, tall, pltpu.VMEM((2, N, N), F32), pltpu.VMEM((2, N, N), F32),
            small, small, small, small, small, small, pltpu.VMEM((N, 2 * N), F32),
            pltpu.SemaphoreType.DMA((2,)), pltpu.SemaphoreType.DMA((2, 8)),
        ],
        compiler_params=pltpu.CompilerParams(vmem_limit_bytes=32 << 20),
    )(sums, panel, next_panel)
    return q, r, coupling, trailing


def solution(mesh):
    return jax.shard_map(
        shards,
        mesh=mesh,
        in_specs=(P(("row", "col"), None), P(("row", "col"), None)),
        out_specs=(P(("row", "col"), None), P(), P(), P(("row", "col"), None)),
        check_vma=False,
    )
```

```python
import functools

import jax
import jax.numpy as jnp
from jax import lax
from jax.experimental import pallas as pl
from jax.experimental.pallas import tpu as pltpu
from jax.sharding import PartitionSpec as P

MESH = pl.DeviceIdType.MESH
F32 = jnp.float32
BF16 = jnp.bfloat16
HIGHEST = lax.Precision.HIGHEST
N = 128
T = N // 8
HALF = T // 2
ROW_X = 4
ROW_Y = 8
COL_K = 2
COL_Z = 8
CHUNKS = ROW_X * COL_K
HI, LO, CO, DG, USED, PADDED = 0, 8, 16, 32, 34, 40


def two_sum(a, b):
    s = a + b
    t = s - a
    return s, (a - (s - t)) + (b - t)


def quick_sum(a, b):
    s = a + b
    return s, b - (s - a)


def unit(x):
    q = x * (2.0**23 + 1.0)
    return jnp.abs(q - q * (1.0 - 2.0**-24))


def pieces(x, sigma):
    s1 = (x + sigma) - sigma
    x = x - s1
    sigma = sigma * 2.0**-8
    s2 = (x + sigma) - sigma
    x = x - s2
    sigma = sigma * 2.0**-8
    s3 = (x + sigma) - sigma
    return s1.astype(BF16), s2.astype(BF16), s3.astype(BF16), (x - s3).astype(BF16)


def split3(x):
    a = x.astype(BF16)
    x = x - a.astype(F32)
    b = x.astype(BF16)
    return a, b, (x - b.astype(F32)).astype(BF16)


def tdot(a, b):
    return lax.dot_general(a, b, (((0,), (0,)), ((), ())), preferred_element_type=F32)


def dot(a, b, dims=((1,), (0,))):
    return lax.dot_general(a, b, (dims, ((), ())), precision=HIGHEST, preferred_element_type=F32)


def dot3(a, b, dims=((1,), (0,))):
    a1, b1 = a.astype(BF16), b.astype(BF16)
    a2, b2 = (a - a1.astype(F32)).astype(BF16), (b - b1.astype(F32)).astype(BF16)
    left = jnp.concatenate([a1, a1, a2], dims[0][0])
    right = jnp.concatenate([b1, b2, b1], dims[1][0])
    return lax.dot_general(left, right, (dims, ((), ())), preferred_element_type=F32)


def lane_sub():
    shape = (8, N)
    return lax.broadcasted_iota(jnp.int32, shape, 1), lax.broadcasted_iota(jnp.int32, shape, 0)


def fold(top, low, i):
    lane, sub = lane_sub()
    off = lane - 8 * i
    far = lane - 8 * (T - 1 - i)
    left = pltpu.roll(low, (8 * i + 8) % N, 1)
    block = pltpu.roll(low, (16 * i + 8) % N, 1)
    tile = jnp.where(off > sub, jnp.where(off < 8, block, left), top)
    diag = jnp.sum(jnp.where(far == sub, low, 0.0), axis=0, keepdims=True)
    return tile, diag


def unfold(tile, diag, i):
    lane, sub = lane_sub()
    off = lane - 8 * i
    far = lane - 8 * (T - 1 - i)
    top = jnp.where(off <= sub, tile, 0.0)
    left = pltpu.roll(tile, (N - 8 * i - 8) % N, 1)
    block = pltpu.roll(tile, (N - 16 * i - 8) % N, 1)
    low = jnp.where(far == sub, diag, jnp.where((far > sub) & (far < 8), block, 0.0))
    return top, jnp.where(far < 0, left, low)


def merge(slots):
    n = slots.shape[0]

    def pair(h, l, rows):
        hs, ls = slots[0, pl.ds(h, rows)], slots[0, pl.ds(l, rows)]
        for j in range(1, n):
            hs, e = two_sum(hs, slots[j, pl.ds(h, rows)])
            ls = ls + (slots[j, pl.ds(l, rows)] + e)
        return quick_sum(hs, ls)

    hi, lo = pair(HI, LO, 8)
    dh, dl = pair(DG, DG + 1, 1)
    co = slots[0, pl.ds(CO, 16)]
    for j in range(1, n):
        co = co + slots[j, pl.ds(CO, 16)]
    return hi, lo, co, dh, dl


def put(ref, parts):
    hi, lo, co, dh, dl = parts
    ref[pl.ds(HI, 8)] = hi
    ref[pl.ds(LO, 8)] = lo
    ref[pl.ds(CO, 16)] = co
    ref[pl.ds(DG, 1)] = dh
    ref[pl.ds(DG + 1, 1)] = dl


def sums_kernel(
    panel_hbm, next_hbm, out_ref,
    panel, nxt, ps, first, got1, mine1, got2, mine2, got3, mine3, got4, in_sem, send_sem, recv_sem,
):
    rows = panel.shape[0]
    step = 1024
    loads = []
    for i in range(0, rows, step):
        pair = []
        for j, (src, dst) in enumerate(((panel_hbm, panel), (next_hbm, nxt))):
            for h in range(2):
                at = pl.ds(i + h * (step // 2), step // 2)
                pair.append(pltpu.make_async_copy(src.at[at], dst.at[at], in_sem.at[j, 2 * (i // step) + h]))
                pair[-1].start()
        loads.append(pair)
    r, c = lax.axis_index("row"), lax.axis_index("col")
    y, x = lax.div(r, ROW_X), lax.rem(r, ROW_X)
    z, k = lax.div(c, COL_K), lax.rem(c, COL_K)
    g = x * COL_K + k

    def near(i):
        return (y * ROW_X + lax.div(i, COL_K), z * COL_K + lax.rem(i, COL_K))

    def along_z(i):
        return (r, i * COL_K + k)

    def along_y(i):
        return (i * ROW_X + x, c)

    groups = ((CHUNKS, g, near), (COL_Z, z, along_z), (ROW_Y, y, along_y))
    barrier = pltpu.get_barrier_semaphore()
    for n, me, at in groups:
        for j in range(1, n):
            pl.semaphore_signal(barrier, inc=1, device_id=at(lax.rem(me + j, n)), device_id_type=MESH)

    hi = lo = jnp.zeros((N, N), F32)
    low = cross = jnp.zeros((N, N), F32)
    block = 128
    for i in range(0, rows, step):
        for copy in loads[i // step]:
            copy.wait()
        m = jnp.zeros((8, N), F32)
        for j in range(0, step, block):
            v = jnp.abs(panel[pl.ds(i + j, block), :])
            m = jnp.maximum(m, jnp.max(v.reshape(block // 8, 8, N), axis=0))
        sigma = unit(jnp.max(m, axis=0, keepdims=True)) * (1.5 * 2.0**17)
        for j in range(0, step, block):
            at = pl.ds(i + j, block)
            for n, s in enumerate(pieces(panel[at, :], sigma) + split3(nxt[at, :])):
                ps[at, pl.ds(n * N, N)] = s
        at = pl.ds(i, step)
        e = tdot(ps[at, 0:2 * N], ps[at, :])
        w = tdot(ps[at, 2 * N:4 * N], ps[at, 4 * N:6 * N])
        hi, err = two_sum(hi, e[:N, :N])
        lo = lo + err
        hi, err = two_sum(hi, e[:N, N:2 * N] + e[N:, :N])
        lo = lo + err + e[N:, N:2 * N]
        low = low + ((e[:N, 2 * N:3 * N] + e[:N, 3 * N:4 * N]) + (e[N:, 2 * N:3 * N] + e[N:, 3 * N:4 * N]))
        part = (e[:N, 6 * N:] + e[N:, 6 * N:]) + ((w[:N, :N] + w[:N, N:]) + w[N:, :N])
        part = part + ((e[:N, 5 * N:6 * N] + e[N:, 4 * N:5 * N]) + e[N:, 5 * N:6 * N])
        cross = cross + (e[:N, 4 * N:5 * N] + part)
    lo = lo + (low + low.T)
    hi, lo = quick_sum(hi, lo)
    for i in range(CHUNKS):
        a, b = slice(8 * i, 8 * i + 8), slice(8 * (T - 1 - i), 8 * (T - i))
        ht, hd = fold(hi[a], hi[b], i)
        lt, ld = fold(lo[a], lo[b], i)
        put(first.at[i], (ht, lt, cross[16 * i:16 * i + 16], hd, ld))

    pl.semaphore_wait(barrier, sum(n - 1 for n, _, _ in groups))

    def spread(phase, group, source, target):
        n, me, at = group
        for j in range(1, n):
            to = lax.rem(me + j, n)
            pltpu.make_async_remote_copy(
                source(to).at[pl.ds(0, USED)], target(j).at[pl.ds(0, USED)],
                send_sem.at[phase], recv_sem.at[phase], device_id=at(to), device_id_type=MESH,
            ).start()

    def arrived(sem, phase, n):
        whole = first.at[pl.ds(0, n - 1), pl.ds(0, USED)]
        pltpu.make_async_copy(whole, whole, sem.at[phase]).wait()

    spread(0, groups[0], lambda to: first.at[to], lambda j: got1.at[CHUNKS - j])
    got1[0] = first[g]
    arrived(recv_sem, 0, CHUNKS)
    put(mine1, merge(got1))
    spread(1, groups[1], lambda to: mine1, lambda j: got2.at[z])
    got2[z] = mine1[...]
    arrived(recv_sem, 1, COL_Z)
    put(mine2, merge(got2))
    spread(2, groups[2], lambda to: mine2, lambda j: got3.at[y])
    got3[y] = mine2[...]
    arrived(recv_sem, 2, ROW_Y)
    put(mine3, merge(got3))
    spread(3, groups[0], lambda to: mine3, lambda j: got4.at[g])
    got4[g] = mine3[...]
    arrived(recv_sem, 3, CHUNKS)
    out_ref[...] = got4[...]
    for phase, n in enumerate((CHUNKS, COL_Z, ROW_Y, CHUNKS)):
        arrived(send_sem, phase, n)


def lanes(v, i):
    return jnp.broadcast_to(v[:, i:i + 1], (8, N))


def subs(v, i):
    return jnp.broadcast_to(v[i:i + 1, :], (8, N))


def factor(gram, upper, lower_inv):
    lane, sub = lane_sub()
    a = [gram[8 * b:8 * b + 8, :] for b in range(T)]
    t = [lanes(a[0], i) for i in range(8)]
    for b in range(T):
        off = lane - 8 * b
        inside = (off >= 0) & (off < 8)
        d = {(i, j): subs(t[j], i) for i in range(8) for j in range(i, 8)}
        rs, h = [], {}
        for i in range(8):
            rs.append(lax.rsqrt(d[i, i]))
            for j in range(i + 1, 8):
                h[i, j] = rs[i] * d[i, j]
            for k in range(i + 1, 8):
                for j in range(k, 8):
                    d[k, j] = d[k, j] - h[i, k] * h[i, j]
        ahead = f2 = None
        if b + 1 < T:
            ahead = [lanes(a[b + 1], 8 * (b + 1) + j) for j in range(8)]
            f2 = [lanes(a[b + 1], 8 * b + i) for i in range(8)]
            for i in range(8):
                f2[i] = f2[i] * rs[i]
                for j in range(i + 1, 8):
                    f2[j] = f2[j] - f2[i] * h[i, j]
                for j in range(8):
                    ahead[j] = ahead[j] - f2[i] * subs(f2[i], j)
        v = jnp.where(inside, jnp.where(off == sub, 1.0, 0.0), a[b])
        g = []
        scale = rs[0]
        for i in range(8):
            if i:
                scale = jnp.where(sub == i, rs[i], scale)
            g.append(rs[i] * subs(v, i))
            if i < 7:
                below = jnp.where(sub > i, t[i] * rs[i], 0.0)
                v = v - below * g[i]
                for j in range(i + 1, 8):
                    t[j] = t[j] - below * h[i, j]
        lower_inv[8 * b:8 * b + 8, :] = jnp.where(off < 8, v * scale, 0.0)
        u = v
        for j in range(8):
            u = jnp.where(off == j, jnp.where(sub <= j, t[j], 0.0), u)
        upper[8 * b:8 * b + 8, :] = jnp.where(off < 0, 0.0, u * scale)
        for b2 in range(b + 1, T):
            if b2 > b + 1:
                f2 = [lanes(a[b2], 8 * b + i) for i in range(8)]
            v2 = jnp.where(inside, 0.0, a[b2])
            for i in range(8):
                if b2 > b + 1:
                    f2[i] = f2[i] * rs[i]
                    for j in range(i + 1, 8):
                        f2[j] = f2[j] - f2[i] * h[i, j]
                v2 = v2 - f2[i] * g[i]
            a[b2] = v2
        t = ahead


def finish_kernel(
    sums, panel_hbm, next_hbm, q_hbm, r_ref, coupling_ref, trailing_hbm,
    panel, nxt, q, trail, hi_ref, lo_ref, gram, r1, x1, gram2, r2, x2, in_sem, out_sem, *, count,
):
    rows = panel.shape[0]
    block = 256
    loads = []
    for i in range(0, rows, block):
        at = pl.ds(i, block)
        for j, (src, dst) in enumerate(((panel_hbm, panel), (next_hbm, nxt))):
            loads.append(pltpu.make_async_copy(src.at[at], dst.at[at], in_sem.at[j, i // block]))
            loads[-1].start()
    for i in range(HALF):
        a, b = slice(8 * i, 8 * i + 8), slice(8 * (T - 1 - i), 8 * (T - i))
        for ref, at, dg in ((hi_ref, HI, DG), (lo_ref, LO, DG + 1)):
            ref[a, :], ref[b, :] = unfold(sums[i, pl.ds(at, 8)], sums[i, pl.ds(dg, 1)], i)
    row_id = lax.broadcasted_iota(jnp.int32, (N, N), 0)
    col_id = lax.broadcasted_iota(jnp.int32, (N, N), 1)
    eye = row_id == col_id

    def whole(ref):
        half = ref[...]
        return jnp.where(eye, half, half + half.T) * (1.0 / count)

    hi, lo = whole(hi_ref), whole(lo_ref)
    diag = jnp.where(eye, hi, 0.0)
    s_row = unit(lax.rsqrt(jnp.sum(diag, axis=0, keepdims=True)))
    s_col = unit(lax.rsqrt(jnp.sum(diag, axis=1, keepdims=True)))
    hi = hi * s_row * s_col
    lo = lo * s_row * s_col
    gram[...] = hi
    factor(gram, r1, x1)
    s1, s2, s3, s4 = pieces(r1[...], 1.5 * 2.0**15)
    p12, p34 = jnp.concatenate([s1, s2], 1), jnp.concatenate([s3, s4], 1)
    e = tdot(p12, jnp.concatenate([p12, p34], 1))
    low = (e[:N, 2 * N:3 * N] + e[:N, 3 * N:]) + (e[N:, 2 * N:3 * N] + e[N:, 3 * N:])
    low = (low + low.T) + e[N:, N:2 * N]
    rest, e1 = two_sum(hi, -e[:N, :N])
    rest, e2 = two_sum(rest, -(e[:N, N:2 * N] + e[N:, :N]))
    rest = rest + ((e1 + e2) + (lo - low))
    x = x1[...]
    m = dot(x, r1[...], ((1,), (1,)))
    y = dot3(x, rest)
    gram2[...] = dot(m, m, ((1,), (1,))) + dot3(y, x, ((1,), (1,)))
    factor(gram2, r2, x2)
    w = dot(x, x2[...], ((0,), (1,))) * s_col
    cross = jnp.concatenate([sums[i, pl.ds(CO, 16)] for i in range(CHUNKS)], 0) * (1.0 / count)
    coupling = dot(w, cross, ((0,), (0,)))
    coupling_ref[...] = coupling
    for copy in loads:
        copy.wait()
    copies = []

    def send(src, dst, j, i):
        at = pl.ds(i, block)
        copies.append(pltpu.make_async_copy(src.at[at], dst.at[at], out_sem.at[j, i // block]))
        copies[-1].start()

    for i in range(0, rows, block):
        q[pl.ds(i, block), :] = dot(panel[pl.ds(i, block), :], w)
        send(q, q_hbm, 0, i)
    back = dot(w, coupling)
    for i in range(0, rows, block):
        at = pl.ds(i, block)
        trail[at, :] = nxt[at, :] - dot(panel[at, :], back)
        send(trail, trailing_hbm, 1, i)
    r_ref[...] = dot(r2[...], r1[...]) / s_row
    for copy in copies:
        copy.wait()


def shards(panel, next_panel):
    rows = panel.shape[0]
    count = rows * lax.axis_size("row") * lax.axis_size("col")
    hbm, vmem = pl.BlockSpec(memory_space=pltpu.HBM), pl.BlockSpec(memory_space=pltpu.VMEM)
    small = pltpu.VMEM((N, N), F32)
    tall = pltpu.VMEM((rows, N), F32)
    slots = pltpu.VMEM((CHUNKS, PADDED, N), F32)
    one = pltpu.VMEM((PADDED, N), F32)
    sums = pl.pallas_call(
        sums_kernel,
        name="sums",
        out_shape=jax.ShapeDtypeStruct((CHUNKS, PADDED, N), F32),
        in_specs=[hbm, hbm],
        out_specs=vmem,
        scratch_shapes=[
            tall, tall, pltpu.VMEM((rows, 7 * N), BF16),
            slots, slots, one, slots, one, slots, one, slots,
            pltpu.SemaphoreType.DMA((2, 4)), pltpu.SemaphoreType.DMA((4,)), pltpu.SemaphoreType.DMA((4,)),
        ],
        compiler_params=pltpu.CompilerParams(collective_id=0, has_side_effects=True, vmem_limit_bytes=63 << 20),
    )(panel, next_panel)
    big = jax.ShapeDtypeStruct((rows, N), F32)
    little = jax.ShapeDtypeStruct((N, N), F32)
    q, r, coupling, trailing = pl.pallas_call(
        functools.partial(finish_kernel, count=count),
        name="finish",
        out_shape=(big, little, little, big),
        in_specs=[vmem, hbm, hbm],
        out_specs=(hbm, vmem, vmem, hbm),
        scratch_shapes=[
            tall, tall, tall, tall, small, small, small, small, small, small, small, small,
            pltpu.SemaphoreType.DMA((2, 8)), pltpu.SemaphoreType.DMA((2, 8)),
        ],
        compiler_params=pltpu.CompilerParams(vmem_limit_bytes=63 << 20),
    )(sums, panel, next_panel)
    return q, r, coupling, trailing


def solution(mesh):
    return jax.shard_map(
        shards,
        mesh=mesh,
        in_specs=(P(("row", "col"), None), P(("row", "col"), None)),
        out_specs=(P(("row", "col"), None), P(), P(), P(("row", "col"), None)),
        check_vma=False,
    )
```

```python
import functools

import jax
import jax.numpy as jnp
from jax import lax
from jax.experimental import pallas as pl
from jax.experimental.pallas import tpu as pltpu
from jax.sharding import PartitionSpec as P

MESH = pl.DeviceIdType.MESH
F32 = jnp.float32
BF16 = jnp.bfloat16
HIGHEST = lax.Precision.HIGHEST
N = 128
T = N // 8
HALF = T // 2
ROW_X = 4
ROW_Y = 8
COL_K = 2
COL_Z = 8
CHUNKS = ROW_X * COL_K
HI, LO, DG, USED, PADDED = 0, 8, 16, 18, 24
CROSS = N // CHUNKS


def two_sum(a, b):
    s = a + b
    t = s - a
    return s, (a - (s - t)) + (b - t)


def quick_sum(a, b):
    s = a + b
    return s, b - (s - a)


def unit(x):
    q = x * (2.0**23 + 1.0)
    return jnp.abs(q - q * (1.0 - 2.0**-24))


def pieces(x, sigma):
    s1 = (x + sigma) - sigma
    x = x - s1
    sigma = sigma * 2.0**-8
    s2 = (x + sigma) - sigma
    x = x - s2
    sigma = sigma * 2.0**-8
    s3 = (x + sigma) - sigma
    return s1.astype(BF16), s2.astype(BF16), s3.astype(BF16), (x - s3).astype(BF16)


def split3(x):
    a = x.astype(BF16)
    x = x - a.astype(F32)
    b = x.astype(BF16)
    return a, b, (x - b.astype(F32)).astype(BF16)


def tdot(a, b):
    return lax.dot_general(a, b, (((0,), (0,)), ((), ())), preferred_element_type=F32)


def dot(a, b, dims=((1,), (0,))):
    return lax.dot_general(a, b, (dims, ((), ())), precision=HIGHEST, preferred_element_type=F32)


def dot3(a, b, dims=((1,), (0,))):
    a1, b1 = a.astype(BF16), b.astype(BF16)
    a2, b2 = (a - a1.astype(F32)).astype(BF16), (b - b1.astype(F32)).astype(BF16)
    left = jnp.concatenate([a1, a1, a2], dims[0][0])
    right = jnp.concatenate([b1, b2, b1], dims[1][0])
    return lax.dot_general(left, right, (dims, ((), ())), preferred_element_type=F32)


def lane_sub():
    shape = (8, N)
    return lax.broadcasted_iota(jnp.int32, shape, 1), lax.broadcasted_iota(jnp.int32, shape, 0)


def fold(top, low, i):
    lane, sub = lane_sub()
    off = lane - 8 * i
    far = lane - 8 * (T - 1 - i)
    left = pltpu.roll(low, (8 * i + 8) % N, 1)
    block = pltpu.roll(low, (16 * i + 8) % N, 1)
    tile = jnp.where(off > sub, jnp.where(off < 8, block, left), top)
    diag = jnp.sum(jnp.where(far == sub, low, 0.0), axis=0, keepdims=True)
    return tile, diag


def unfold(tile, diag, i):
    lane, sub = lane_sub()
    off = lane - 8 * i
    far = lane - 8 * (T - 1 - i)
    top = jnp.where(off <= sub, tile, 0.0)
    left = pltpu.roll(tile, (N - 8 * i - 8) % N, 1)
    block = pltpu.roll(tile, (N - 16 * i - 8) % N, 1)
    low = jnp.where(far == sub, diag, jnp.where((far > sub) & (far < 8), block, 0.0))
    return top, jnp.where(far < 0, left, low)


def merge(slots, out):
    def pair(h, l, rows):
        hs, ls = slots[0, pl.ds(h, rows)], slots[0, pl.ds(l, rows)]
        for j in range(1, slots.shape[0]):
            hs, e = two_sum(hs, slots[j, pl.ds(h, rows)])
            ls = ls + (slots[j, pl.ds(l, rows)] + e)
        out[pl.ds(h, rows)], out[pl.ds(l, rows)] = quick_sum(hs, ls)

    pair(HI, LO, 8)
    pair(DG, DG + 1, 1)


def plain_merge(slots, out):
    total = slots[0]
    for j in range(1, slots.shape[0]):
        total = total + slots[j]
    out[...] = total


def sums_kernel(
    panel_hbm, next_hbm, gram_ref, cross_ref, panel, nxt, ps,
    gram0, gram1, gram2, gram3, gram4, own1, own2, own3,
    cross0, cross1, cross2, cross3, cross4, part1, part2, part3, in_sem, send_sem, recv_sem,
):
    rows = panel.shape[0]
    step = 1024
    loads = []
    for i in range(0, rows, step):
        pair = []
        for j, (src, dst) in enumerate(((panel_hbm, panel), (next_hbm, nxt))):
            for h in range(2):
                at = pl.ds(i + h * (step // 2), step // 2)
                pair.append(pltpu.make_async_copy(src.at[at], dst.at[at], in_sem.at[j, 2 * (i // step) + h]))
                pair[-1].start()
        loads.append(pair)
    r, c = lax.axis_index("row"), lax.axis_index("col")
    y, x = lax.div(r, ROW_X), lax.rem(r, ROW_X)
    z, k = lax.div(c, COL_K), lax.rem(c, COL_K)
    g = x * COL_K + k

    def near(i):
        return (y * ROW_X + lax.div(i, COL_K), z * COL_K + lax.rem(i, COL_K))

    def along_z(i):
        return (r, i * COL_K + k)

    def along_y(i):
        return (i * ROW_X + x, c)

    groups = ((CHUNKS, g, near), (COL_Z, z, along_z), (ROW_Y, y, along_y))
    barrier = pltpu.get_barrier_semaphore()
    for n, me, at in groups:
        for j in range(1, n):
            pl.semaphore_signal(barrier, inc=1, device_id=at(lax.rem(me + j, n)), device_id_type=MESH)

    hi = lo = jnp.zeros((N, N), F32)
    low = jnp.zeros((N, N), F32)
    block = 128
    for i in range(0, rows, step):
        for copy in loads[i // step][:2]:
            copy.wait()
        m = jnp.zeros((8, N), F32)
        for j in range(0, step, block):
            v = jnp.abs(panel[pl.ds(i + j, block), :])
            m = jnp.maximum(m, jnp.max(v.reshape(block // 8, 8, N), axis=0))
        sigma = unit(jnp.max(m, axis=0, keepdims=True)) * (1.5 * 2.0**17)
        for j in range(0, step, block):
            at = pl.ds(i + j, block)
            for n, s in enumerate(pieces(panel[at, :], sigma)):
                ps[at, pl.ds(n * N, N)] = s
        at = pl.ds(i, step)
        e = tdot(ps[at, 0:2 * N], ps[at, 0:4 * N])
        hi, err = two_sum(hi, e[:N, :N])
        lo = lo + err
        hi, err = two_sum(hi, e[:N, N:2 * N] + e[N:, :N])
        lo = lo + err + e[N:, N:2 * N]
        low = low + ((e[:N, 2 * N:3 * N] + e[:N, 3 * N:4 * N]) + (e[N:, 2 * N:3 * N] + e[N:, 3 * N:4 * N]))
    lo = lo + (low + low.T)
    hi, lo = quick_sum(hi, lo)
    for i in range(CHUNKS):
        a, b = slice(8 * i, 8 * i + 8), slice(8 * (T - 1 - i), 8 * (T - i))
        ht, hd = fold(hi[a], hi[b], i)
        lt, ld = fold(lo[a], lo[b], i)
        gram0[i, pl.ds(HI, 8)] = ht
        gram0[i, pl.ds(LO, 8)] = lt
        gram0[i, pl.ds(DG, 1)] = hd
        gram0[i, pl.ds(DG + 1, 1)] = ld

    pl.semaphore_wait(barrier, sum(n - 1 for n, _, _ in groups))

    def spread(stream, phase, group, source, target, used):
        n, me, at = group
        for j in range(1, n):
            to = lax.rem(me + j, n)
            pltpu.make_async_remote_copy(
                source(to).at[pl.ds(0, used)], target(j).at[pl.ds(0, used)],
                send_sem.at[stream, phase], recv_sem.at[stream, phase], device_id=at(to), device_id_type=MESH,
            ).start()

    def arrived(sem, stream, phase, n):
        whole = (gram0.at[pl.ds(0, n - 1), pl.ds(0, USED)], cross0.at[pl.ds(0, n - 1)])[stream]
        pltpu.make_async_copy(whole, whole, sem.at[stream, phase]).wait()

    class Stream:
        def __init__(self, stream, first, slots, own, add, used):
            self.stream, self.first, self.slots, self.own, self.add, self.used = stream, first, slots, own, add, used

        def scatter(self):
            spread(self.stream, 0, groups[0], lambda to: self.first.at[to], lambda j: self.slots[0].at[CHUNKS - j], self.used)
            self.slots[0][0] = self.first[g]

        def forward(self, phase):
            group = groups[(phase + 1) % 3]
            slot = group[1]
            arrived(recv_sem, self.stream, phase, groups[phase][0])
            own = self.own[phase]
            self.add(self.slots[phase], own)
            spread(self.stream, phase + 1, group, lambda to: own, lambda j: self.slots[phase + 1].at[slot], self.used)
            self.slots[phase + 1][slot] = own[...]

    gram = Stream(0, gram0, (gram1, gram2, gram3, gram4), (own1, own2, own3), merge, USED)
    cross = Stream(1, cross0, (cross1, cross2, cross3, cross4), (part1, part2, part3), plain_merge, CROSS)
    gram.scatter()
    total = jnp.zeros((N, N), F32)
    for i in range(0, rows, step):
        for copy in loads[i // step][2:]:
            copy.wait()
        for j in range(0, step, block):
            at = pl.ds(i + j, block)
            for n, s in enumerate(split3(nxt[at, :])):
                ps[at, pl.ds((4 + n) * N, N)] = s
        at = pl.ds(i, step)
        e = tdot(ps[at, 0:2 * N], ps[at, 4 * N:7 * N])
        w = tdot(ps[at, 2 * N:4 * N], ps[at, 4 * N:6 * N])
        part = (e[:N, 2 * N:] + e[N:, 2 * N:]) + ((w[:N, :N] + w[:N, N:]) + w[N:, :N])
        part = part + ((e[:N, N:2 * N] + e[N:, :N]) + e[N:, N:2 * N])
        total = total + (e[:N, :N] + part)
    for i in range(CHUNKS):
        cross0[i] = total[CROSS * i:CROSS * (i + 1)]
    cross.scatter()
    for phase in range(3):
        gram.forward(phase)
        cross.forward(phase)
    arrived(recv_sem, 0, 3, CHUNKS)
    gram_ref[...] = gram4[...]
    arrived(recv_sem, 1, 3, CHUNKS)
    cross_ref[...] = cross4[...]
    for stream in range(2):
        for phase, n in enumerate((CHUNKS, COL_Z, ROW_Y, CHUNKS)):
            arrived(send_sem, stream, phase, n)


def lanes(v, i):
    return jnp.broadcast_to(v[:, i:i + 1], (8, N))


def subs(v, i):
    return jnp.broadcast_to(v[i:i + 1, :], (8, N))


def factor(gram, upper, lower_inv):
    lane, sub = lane_sub()
    a = [gram[8 * b:8 * b + 8, :] for b in range(T)]
    t = [lanes(a[0], i) for i in range(8)]
    for b in range(T):
        off = lane - 8 * b
        inside = (off >= 0) & (off < 8)
        d = {(i, j): subs(t[j], i) for i in range(8) for j in range(i, 8)}
        rs, h = [], {}
        for i in range(8):
            rs.append(lax.rsqrt(d[i, i]))
            for j in range(i + 1, 8):
                h[i, j] = rs[i] * d[i, j]
            for k in range(i + 1, 8):
                for j in range(k, 8):
                    d[k, j] = d[k, j] - h[i, k] * h[i, j]
        ahead = f2 = None
        if b + 1 < T:
            ahead = [lanes(a[b + 1], 8 * (b + 1) + j) for j in range(8)]
            f2 = [lanes(a[b + 1], 8 * b + i) for i in range(8)]
            for i in range(8):
                f2[i] = f2[i] * rs[i]
                for j in range(i + 1, 8):
                    f2[j] = f2[j] - f2[i] * h[i, j]
                for j in range(8):
                    ahead[j] = ahead[j] - f2[i] * subs(f2[i], j)
        v = jnp.where(inside, jnp.where(off == sub, 1.0, 0.0), a[b])
        g = []
        scale = rs[0]
        for i in range(8):
            if i:
                scale = jnp.where(sub == i, rs[i], scale)
            g.append(rs[i] * subs(v, i))
            if i < 7:
                below = jnp.where(sub > i, t[i] * rs[i], 0.0)
                v = v - below * g[i]
                for j in range(i + 1, 8):
                    t[j] = t[j] - below * h[i, j]
        lower_inv[8 * b:8 * b + 8, :] = jnp.where(off < 8, v * scale, 0.0)
        u = v
        for j in range(8):
            u = jnp.where(off == j, jnp.where(sub <= j, t[j], 0.0), u)
        upper[8 * b:8 * b + 8, :] = jnp.where(off < 0, 0.0, u * scale)
        for b2 in range(b + 1, T):
            if b2 > b + 1:
                f2 = [lanes(a[b2], 8 * b + i) for i in range(8)]
            v2 = jnp.where(inside, 0.0, a[b2])
            for i in range(8):
                if b2 > b + 1:
                    f2[i] = f2[i] * rs[i]
                    for j in range(i + 1, 8):
                        f2[j] = f2[j] - f2[i] * h[i, j]
                v2 = v2 - f2[i] * g[i]
            a[b2] = v2
        t = ahead


def finish_kernel(
    sums, cross_sum, panel_hbm, next_hbm, q_hbm, r_ref, coupling_ref, trailing_hbm,
    panel, nxt, q, trail, hi_ref, lo_ref, gram, r1, x1, gram2, r2, x2, in_sem, out_sem, *, count,
):
    rows = panel.shape[0]
    block = 256
    loads = []
    for i in range(0, rows, block):
        at = pl.ds(i, block)
        for j, (src, dst) in enumerate(((panel_hbm, panel), (next_hbm, nxt))):
            loads.append(pltpu.make_async_copy(src.at[at], dst.at[at], in_sem.at[j, i // block]))
            loads[-1].start()
    for i in range(HALF):
        a, b = slice(8 * i, 8 * i + 8), slice(8 * (T - 1 - i), 8 * (T - i))
        for ref, at, dg in ((hi_ref, HI, DG), (lo_ref, LO, DG + 1)):
            ref[a, :], ref[b, :] = unfold(sums[i, pl.ds(at, 8)], sums[i, pl.ds(dg, 1)], i)
    row_id = lax.broadcasted_iota(jnp.int32, (N, N), 0)
    col_id = lax.broadcasted_iota(jnp.int32, (N, N), 1)
    eye = row_id == col_id

    def whole(ref):
        half = ref[...]
        return jnp.where(eye, half, half + half.T) * (1.0 / count)

    hi, lo = whole(hi_ref), whole(lo_ref)
    diag = jnp.where(eye, hi, 0.0)
    s_row = unit(lax.rsqrt(jnp.sum(diag, axis=0, keepdims=True)))
    s_col = unit(lax.rsqrt(jnp.sum(diag, axis=1, keepdims=True)))
    hi = hi * s_row * s_col
    lo = lo * s_row * s_col
    gram[...] = hi
    factor(gram, r1, x1)
    s1, s2, s3, s4 = pieces(r1[...], 1.5 * 2.0**15)
    p12, p34 = jnp.concatenate([s1, s2], 1), jnp.concatenate([s3, s4], 1)
    e = tdot(p12, jnp.concatenate([p12, p34], 1))
    low = (e[:N, 2 * N:3 * N] + e[:N, 3 * N:]) + (e[N:, 2 * N:3 * N] + e[N:, 3 * N:])
    low = (low + low.T) + e[N:, N:2 * N]
    rest, e1 = two_sum(hi, -e[:N, :N])
    rest, e2 = two_sum(rest, -(e[:N, N:2 * N] + e[N:, :N]))
    rest = rest + ((e1 + e2) + (lo - low))
    x = x1[...]
    m = dot(x, r1[...], ((1,), (1,)))
    y = dot3(x, rest)
    gram2[...] = dot(m, m, ((1,), (1,))) + dot3(y, x, ((1,), (1,)))
    factor(gram2, r2, x2)
    w = dot(x, x2[...], ((0,), (1,))) * s_col
    cross = cross_sum[...].reshape(N, N) * (1.0 / count)
    coupling = dot(w, cross, ((0,), (0,)))
    coupling_ref[...] = coupling
    for copy in loads:
        copy.wait()
    copies = []

    def send(src, dst, j, i):
        at = pl.ds(i, block)
        copies.append(pltpu.make_async_copy(src.at[at], dst.at[at], out_sem.at[j, i // block]))
        copies[-1].start()

    for i in range(0, rows, block):
        q[pl.ds(i, block), :] = dot(panel[pl.ds(i, block), :], w)
        send(q, q_hbm, 0, i)
    back = dot(w, coupling)
    for i in range(0, rows, block):
        at = pl.ds(i, block)
        trail[at, :] = nxt[at, :] - dot(panel[at, :], back)
        send(trail, trailing_hbm, 1, i)
    r_ref[...] = dot(r2[...], r1[...]) / s_row
    for copy in copies:
        copy.wait()


def shards(panel, next_panel):
    rows = panel.shape[0]
    count = rows * lax.axis_size("row") * lax.axis_size("col")
    hbm, vmem = pl.BlockSpec(memory_space=pltpu.HBM), pl.BlockSpec(memory_space=pltpu.VMEM)
    small = pltpu.VMEM((N, N), F32)
    tall = pltpu.VMEM((rows, N), F32)
    slots = pltpu.VMEM((CHUNKS, PADDED, N), F32)
    one = pltpu.VMEM((PADDED, N), F32)
    cross_slots = pltpu.VMEM((CHUNKS, CROSS, N), F32)
    cross_one = pltpu.VMEM((CROSS, N), F32)
    gram, cross = pl.pallas_call(
        sums_kernel,
        name="sums",
        out_shape=(jax.ShapeDtypeStruct((CHUNKS, PADDED, N), F32), jax.ShapeDtypeStruct((CHUNKS, CROSS, N), F32)),
        in_specs=[hbm, hbm],
        out_specs=(vmem, vmem),
        scratch_shapes=[
            tall, tall, pltpu.VMEM((rows, 7 * N), BF16),
            *(slots,) * 5, *(one,) * 3, *(cross_slots,) * 5, *(cross_one,) * 3,
            pltpu.SemaphoreType.DMA((2, 4)), pltpu.SemaphoreType.DMA((2, 4)), pltpu.SemaphoreType.DMA((2, 4)),
        ],
        compiler_params=pltpu.CompilerParams(collective_id=0, has_side_effects=True, vmem_limit_bytes=53 << 20),
    )(panel, next_panel)
    big = jax.ShapeDtypeStruct((rows, N), F32)
    little = jax.ShapeDtypeStruct((N, N), F32)
    q, r, coupling, trailing = pl.pallas_call(
        functools.partial(finish_kernel, count=count),
        name="finish",
        out_shape=(big, little, little, big),
        in_specs=[vmem, vmem, hbm, hbm],
        out_specs=(hbm, vmem, vmem, hbm),
        scratch_shapes=[
            tall, tall, tall, tall, small, small, small, small, small, small, small, small,
            pltpu.SemaphoreType.DMA((2, 8)), pltpu.SemaphoreType.DMA((2, 8)),
        ],
        compiler_params=pltpu.CompilerParams(vmem_limit_bytes=53 << 20),
    )(gram, cross, panel, next_panel)
    return q, r, coupling, trailing


def solution(mesh):
    return jax.shard_map(
        shards,
        mesh=mesh,
        in_specs=(P(("row", "col"), None), P(("row", "col"), None)),
        out_specs=(P(("row", "col"), None), P(), P(), P(("row", "col"), None)),
        check_vma=False,
    )
```

```python
import functools

import jax
import jax.numpy as jnp
from jax import lax
from jax.experimental import pallas as pl
from jax.experimental.pallas import tpu as pltpu
from jax.sharding import PartitionSpec as P

MESH = pl.DeviceIdType.MESH
F32 = jnp.float32
BF16 = jnp.bfloat16
HIGHEST = lax.Precision.HIGHEST
N = 128
T = N // 8
HALF = T // 2
ROW_X = 4
ROW_Y = 8
COL_K = 2
COL_Z = 8
CHUNKS = ROW_X * COL_K
HI, LO, DG, USED, PADDED = 0, 8, 16, 18, 24
CROSS = N // CHUNKS


def two_sum(a, b):
    s = a + b
    t = s - a
    return s, (a - (s - t)) + (b - t)


def quick_sum(a, b):
    s = a + b
    return s, b - (s - a)


def unit(x):
    q = x * (2.0**23 + 1.0)
    return jnp.abs(q - q * (1.0 - 2.0**-24))


def pieces(x, sigma):
    s1 = (x + sigma) - sigma
    x = x - s1
    sigma = sigma * 2.0**-8
    s2 = (x + sigma) - sigma
    x = x - s2
    sigma = sigma * 2.0**-8
    s3 = (x + sigma) - sigma
    return s1.astype(BF16), s2.astype(BF16), s3.astype(BF16), (x - s3).astype(BF16)


def split3(x):
    a = x.astype(BF16)
    x = x - a.astype(F32)
    b = x.astype(BF16)
    return a, b, (x - b.astype(F32)).astype(BF16)


def tdot(a, b):
    return lax.dot_general(a, b, (((0,), (0,)), ((), ())), preferred_element_type=F32)


def dot(a, b, dims=((1,), (0,))):
    return lax.dot_general(a, b, (dims, ((), ())), precision=HIGHEST, preferred_element_type=F32)


def dot3(a, b, dims=((1,), (0,))):
    a1, b1 = a.astype(BF16), b.astype(BF16)
    a2, b2 = (a - a1.astype(F32)).astype(BF16), (b - b1.astype(F32)).astype(BF16)
    left = jnp.concatenate([a1, a1, a2], dims[0][0])
    right = jnp.concatenate([b1, b2, b1], dims[1][0])
    return lax.dot_general(left, right, (dims, ((), ())), preferred_element_type=F32)


def weights(w):
    a, b, c = split3(w)
    ab = jnp.concatenate([a, b], 1)
    return jnp.concatenate([ab, ab], 0), jnp.concatenate([c, a], 0)


def tall_dot(cut, pair):
    a = jnp.dot(cut[:, 0:2 * N], pair[0], preferred_element_type=F32)
    b = jnp.dot(cut[:, N:3 * N], pair[1], preferred_element_type=F32)
    return a[:, :N] + (a[:, N:] + b)


def lane_sub():
    shape = (8, N)
    return lax.broadcasted_iota(jnp.int32, shape, 1), lax.broadcasted_iota(jnp.int32, shape, 0)


def fold(top, low, i):
    lane, sub = lane_sub()
    off = lane - 8 * i
    far = lane - 8 * (T - 1 - i)
    left = pltpu.roll(low, (8 * i + 8) % N, 1)
    block = pltpu.roll(low, (16 * i + 8) % N, 1)
    tile = jnp.where(off > sub, jnp.where(off < 8, block, left), top)
    diag = jnp.sum(jnp.where(far == sub, low, 0.0), axis=0, keepdims=True)
    return tile, diag


def unfold(tile, diag, i):
    lane, sub = lane_sub()
    off = lane - 8 * i
    far = lane - 8 * (T - 1 - i)
    top = jnp.where(off <= sub, tile, 0.0)
    left = pltpu.roll(tile, (N - 8 * i - 8) % N, 1)
    block = pltpu.roll(tile, (N - 16 * i - 8) % N, 1)
    low = jnp.where(far == sub, diag, jnp.where((far > sub) & (far < 8), block, 0.0))
    return top, jnp.where(far < 0, left, low)


def merge(slots, out):
    def pair(h, l, rows):
        hs, ls = slots[0, pl.ds(h, rows)], slots[0, pl.ds(l, rows)]
        for j in range(1, slots.shape[0]):
            hs, e = two_sum(hs, slots[j, pl.ds(h, rows)])
            ls = ls + (slots[j, pl.ds(l, rows)] + e)
        out[pl.ds(h, rows)], out[pl.ds(l, rows)] = quick_sum(hs, ls)

    pair(HI, LO, 8)
    pair(DG, DG + 1, 1)


def plain_merge(slots, out):
    total = slots[0]
    for j in range(1, slots.shape[0]):
        total = total + slots[j]
    out[...] = total


def sums_kernel(
    panel_hbm, next_hbm, gram_ref, cross_ref, panel, nxt, ps,
    gram0, gram1, gram2, gram3, gram4, own1, own2, own3,
    cross0, cross1, cross2, cross3, cross4, part1, part2, part3, in_sem, send_sem, recv_sem,
):
    rows = panel.shape[0]
    step = 1024
    loads = [[] for _ in range(0, rows, step)]
    for j, (src, dst) in enumerate(((panel_hbm, panel), (next_hbm, nxt))):
        for i in range(0, rows, step):
            for h in range(2):
                at = pl.ds(i + h * (step // 2), step // 2)
                loads[i // step].append(pltpu.make_async_copy(src.at[at], dst.at[at], in_sem.at[j, 2 * (i // step) + h]))
                loads[i // step][-1].start()
    r, c = lax.axis_index("row"), lax.axis_index("col")
    y, x = lax.div(r, ROW_X), lax.rem(r, ROW_X)
    z, k = lax.div(c, COL_K), lax.rem(c, COL_K)
    g = x * COL_K + k

    def near(i):
        return (y * ROW_X + lax.div(i, COL_K), z * COL_K + lax.rem(i, COL_K))

    def along_z(i):
        return (r, i * COL_K + k)

    def along_y(i):
        return (i * ROW_X + x, c)

    groups = ((CHUNKS, g, near), (COL_Z, z, along_z), (ROW_Y, y, along_y))
    barrier = pltpu.get_barrier_semaphore()
    for n, me, at in groups:
        for j in range(1, n):
            pl.semaphore_signal(barrier, inc=1, device_id=at(lax.rem(me + j, n)), device_id_type=MESH)

    hi = lo = jnp.zeros((N, N), F32)
    low = jnp.zeros((N, N), F32)
    block = 128
    for i in range(0, rows, step):
        for copy in loads[i // step][:2]:
            copy.wait()
        m = jnp.zeros((8, N), F32)
        for j in range(0, step, block):
            v = jnp.abs(panel[pl.ds(i + j, block), :])
            m = jnp.maximum(m, jnp.max(v.reshape(block // 8, 8, N), axis=0))
        sigma = unit(jnp.max(m, axis=0, keepdims=True)) * (1.5 * 2.0**17)
        for j in range(0, step, block):
            at = pl.ds(i + j, block)
            for n, s in enumerate(pieces(panel[at, :], sigma)):
                ps[at, pl.ds(n * N, N)] = s
        at = pl.ds(i, step)
        e = tdot(ps[at, 0:2 * N], ps[at, 0:4 * N])
        hi, err = two_sum(hi, e[:N, :N])
        lo = lo + err
        hi, err = two_sum(hi, e[:N, N:2 * N] + e[N:, :N])
        lo = lo + err + e[N:, N:2 * N]
        low = low + ((e[:N, 2 * N:3 * N] + e[:N, 3 * N:4 * N]) + (e[N:, 2 * N:3 * N] + e[N:, 3 * N:4 * N]))
    lo = lo + (low + low.T)
    hi, lo = quick_sum(hi, lo)
    for i in range(CHUNKS):
        a, b = slice(8 * i, 8 * i + 8), slice(8 * (T - 1 - i), 8 * (T - i))
        ht, hd = fold(hi[a], hi[b], i)
        lt, ld = fold(lo[a], lo[b], i)
        gram0[i, pl.ds(HI, 8)] = ht
        gram0[i, pl.ds(LO, 8)] = lt
        gram0[i, pl.ds(DG, 1)] = hd
        gram0[i, pl.ds(DG + 1, 1)] = ld

    pl.semaphore_wait(barrier, sum(n - 1 for n, _, _ in groups))

    def spread(stream, phase, group, source, target, used):
        n, me, at = group
        for j in sorted(range(1, n), key=lambda j: abs(2 * j - n)):
            to = lax.rem(me + j, n)
            pltpu.make_async_remote_copy(
                source(to).at[pl.ds(0, used)], target(j).at[pl.ds(0, used)],
                send_sem.at[stream, phase], recv_sem.at[stream, phase], device_id=at(to), device_id_type=MESH,
            ).start()

    def arrived(sem, stream, phase, n):
        whole = (gram0.at[pl.ds(0, n - 1), pl.ds(0, USED)], cross0.at[pl.ds(0, n - 1)])[stream]
        pltpu.make_async_copy(whole, whole, sem.at[stream, phase]).wait()

    class Stream:
        def __init__(self, stream, first, slots, own, add, used):
            self.stream, self.first, self.slots, self.own, self.add, self.used = stream, first, slots, own, add, used

        def scatter(self):
            spread(self.stream, 0, groups[0], lambda to: self.first.at[to], lambda j: self.slots[0].at[CHUNKS - j], self.used)
            self.slots[0][0] = self.first[g]

        def forward(self, phase):
            group = groups[(phase + 1) % 3]
            slot = group[1]
            arrived(recv_sem, self.stream, phase, groups[phase][0])
            own = self.own[phase]
            self.add(self.slots[phase], own)
            spread(self.stream, phase + 1, group, lambda to: own, lambda j: self.slots[phase + 1].at[slot], self.used)
            self.slots[phase + 1][slot] = own[...]

    gram = Stream(0, gram0, (gram1, gram2, gram3, gram4), (own1, own2, own3), merge, USED)
    cross = Stream(1, cross0, (cross1, cross2, cross3, cross4), (part1, part2, part3), plain_merge, CROSS)
    gram.scatter()
    total = jnp.zeros((N, N), F32)
    for i in range(0, rows, step):
        for copy in loads[i // step][2:]:
            copy.wait()
        for j in range(0, step, block):
            at = pl.ds(i + j, block)
            for n, s in enumerate(split3(nxt[at, :])):
                ps[at, pl.ds((4 + n) * N, N)] = s
        at = pl.ds(i, step)
        e = tdot(ps[at, 0:2 * N], ps[at, 4 * N:7 * N])
        w = tdot(ps[at, 2 * N:4 * N], ps[at, 4 * N:6 * N])
        part = (e[:N, 2 * N:] + e[N:, 2 * N:]) + ((w[:N, :N] + w[:N, N:]) + w[N:, :N])
        part = part + ((e[:N, N:2 * N] + e[N:, :N]) + e[N:, N:2 * N])
        total = total + (e[:N, :N] + part)
    for i in range(CHUNKS):
        cross0[i] = total[CROSS * i:CROSS * (i + 1)]
    cross.scatter()
    for phase in range(3):
        gram.forward(phase)
        cross.forward(phase)
    arrived(recv_sem, 0, 3, CHUNKS)
    gram_ref[...] = gram4[...]
    arrived(recv_sem, 1, 3, CHUNKS)
    cross_ref[...] = cross4[...]
    for stream in range(2):
        for phase, n in enumerate((CHUNKS, COL_Z, ROW_Y, CHUNKS)):
            arrived(send_sem, stream, phase, n)


def lanes(v, i):
    return jnp.broadcast_to(v[:, i:i + 1], (8, N))


def subs(v, i):
    return jnp.broadcast_to(v[i:i + 1, :], (8, N))


def factor(gram, upper, lower_inv):
    lane, sub = lane_sub()
    a = [gram[8 * b:8 * b + 8, :] for b in range(T)]
    t = [lanes(a[0], i) for i in range(8)]
    for b in range(T):
        off = lane - 8 * b
        inside = (off >= 0) & (off < 8)
        d = {(i, j): subs(t[j], i) for i in range(8) for j in range(i, 8)}
        rs, h = [], {}
        for i in range(8):
            rs.append(lax.rsqrt(d[i, i]))
            for j in range(i + 1, 8):
                h[i, j] = rs[i] * d[i, j]
            for k in range(i + 1, 8):
                for j in range(k, 8):
                    d[k, j] = d[k, j] - h[i, k] * h[i, j]
        ahead = f2 = None
        if b + 1 < T:
            ahead = [lanes(a[b + 1], 8 * (b + 1) + j) for j in range(8)]
            f2 = [lanes(a[b + 1], 8 * b + i) for i in range(8)]
            for i in range(8):
                f2[i] = f2[i] * rs[i]
                for j in range(i + 1, 8):
                    f2[j] = f2[j] - f2[i] * h[i, j]
                for j in range(8):
                    ahead[j] = ahead[j] - f2[i] * subs(f2[i], j)
        v = jnp.where(inside, jnp.where(off == sub, 1.0, 0.0), a[b])
        g = []
        scale = rs[0]
        for i in range(8):
            if i:
                scale = jnp.where(sub == i, rs[i], scale)
            g.append(rs[i] * subs(v, i))
            if i < 7:
                below = jnp.where(sub > i, t[i] * rs[i], 0.0)
                v = v - below * g[i]
                for j in range(i + 1, 8):
                    t[j] = t[j] - below * h[i, j]
        lower_inv[8 * b:8 * b + 8, :] = jnp.where(off < 8, v * scale, 0.0)
        u = v
        for j in range(8):
            u = jnp.where(off == j, jnp.where(sub <= j, t[j], 0.0), u)
        upper[8 * b:8 * b + 8, :] = jnp.where(off < 0, 0.0, u * scale)
        for b2 in range(b + 1, T):
            if b2 > b + 1:
                f2 = [lanes(a[b2], 8 * b + i) for i in range(8)]
            v2 = jnp.where(inside, 0.0, a[b2])
            for i in range(8):
                if b2 > b + 1:
                    f2[i] = f2[i] * rs[i]
                    for j in range(i + 1, 8):
                        f2[j] = f2[j] - f2[i] * h[i, j]
                v2 = v2 - f2[i] * g[i]
            a[b2] = v2
        t = ahead


def finish_kernel(
    sums, cross_sum, panel_hbm, next_hbm, q_hbm, r_ref, coupling_ref, trailing_hbm,
    panel, nxt, q, trail, cut, hi_ref, lo_ref, gram, r1, x1, gram2, r2, x2, in_sem, out_sem, *, count,
):
    rows = panel.shape[0]
    block = 256
    loads = []
    for i in range(0, rows, block):
        at = pl.ds(i, block)
        for j, (src, dst) in enumerate(((panel_hbm, panel), (next_hbm, nxt))):
            loads.append(pltpu.make_async_copy(src.at[at], dst.at[at], in_sem.at[j, i // block]))
            loads[-1].start()
    for i in range(HALF):
        a, b = slice(8 * i, 8 * i + 8), slice(8 * (T - 1 - i), 8 * (T - i))
        for ref, at, dg in ((hi_ref, HI, DG), (lo_ref, LO, DG + 1)):
            ref[a, :], ref[b, :] = unfold(sums[i, pl.ds(at, 8)], sums[i, pl.ds(dg, 1)], i)
    row_id = lax.broadcasted_iota(jnp.int32, (N, N), 0)
    col_id = lax.broadcasted_iota(jnp.int32, (N, N), 1)
    eye = row_id == col_id

    def whole(ref):
        half = ref[...]
        return jnp.where(eye, half, half + half.T) * (1.0 / count)

    hi, lo = whole(hi_ref), whole(lo_ref)
    diag = jnp.where(eye, hi, 0.0)
    s_row = unit(lax.rsqrt(jnp.sum(diag, axis=0, keepdims=True)))
    s_col = unit(lax.rsqrt(jnp.sum(diag, axis=1, keepdims=True)))
    hi = hi * s_row * s_col
    lo = lo * s_row * s_col
    gram[...] = hi
    factor(gram, r1, x1)
    s1, s2, s3, s4 = pieces(r1[...], 1.5 * 2.0**15)
    p12, p34 = jnp.concatenate([s1, s2], 1), jnp.concatenate([s3, s4], 1)
    e = tdot(p12, jnp.concatenate([p12, p34], 1))
    low = (e[:N, 2 * N:3 * N] + e[:N, 3 * N:]) + (e[N:, 2 * N:3 * N] + e[N:, 3 * N:])
    low = (low + low.T) + e[N:, N:2 * N]
    rest, e1 = two_sum(hi, -e[:N, :N])
    rest, e2 = two_sum(rest, -(e[:N, N:2 * N] + e[N:, :N]))
    rest = rest + ((e1 + e2) + (lo - low))
    x = x1[...]
    m = dot(x, r1[...], ((1,), (1,)))
    y = dot3(x, rest)
    gram2[...] = dot(m, m, ((1,), (1,))) + dot3(y, x, ((1,), (1,)))
    factor(gram2, r2, x2)
    w = dot(x, x2[...], ((0,), (1,))) * s_col
    cross = cross_sum[...].reshape(N, N) * (1.0 / count)
    coupling = dot(w, cross, ((0,), (0,)))
    coupling_ref[...] = coupling
    pair = weights(w)
    for copy in loads:
        copy.wait()
    copies = []

    def send(src, dst, j, i):
        at = pl.ds(i, block)
        copies.append(pltpu.make_async_copy(src.at[at], dst.at[at], out_sem.at[j, i // block]))
        copies[-1].start()

    for i in range(0, rows, block):
        at = pl.ds(i, block)
        first, second, third = split3(panel[at, :])
        cut[at, :] = jnp.concatenate([second, first, third], 1)
        q[at, :] = tall_dot(cut[at, :], pair)
        send(q, q_hbm, 0, i)
    back = weights(dot(w, coupling))
    for i in range(0, rows, block):
        at = pl.ds(i, block)
        trail[at, :] = nxt[at, :] - tall_dot(cut[at, :], back)
        send(trail, trailing_hbm, 1, i)
    r_ref[...] = dot(r2[...], r1[...]) / s_row
    for copy in copies:
        copy.wait()


def shards(panel, next_panel):
    rows = panel.shape[0]
    count = rows * lax.axis_size("row") * lax.axis_size("col")
    hbm, vmem = pl.BlockSpec(memory_space=pltpu.HBM), pl.BlockSpec(memory_space=pltpu.VMEM)
    small = pltpu.VMEM((N, N), F32)
    tall = pltpu.VMEM((rows, N), F32)
    slots = pltpu.VMEM((CHUNKS, PADDED, N), F32)
    one = pltpu.VMEM((PADDED, N), F32)
    cross_slots = pltpu.VMEM((CHUNKS, CROSS, N), F32)
    cross_one = pltpu.VMEM((CROSS, N), F32)
    gram, cross = pl.pallas_call(
        sums_kernel,
        name="sums",
        out_shape=(jax.ShapeDtypeStruct((CHUNKS, PADDED, N), F32), jax.ShapeDtypeStruct((CHUNKS, CROSS, N), F32)),
        in_specs=[hbm, hbm],
        out_specs=(vmem, vmem),
        scratch_shapes=[
            tall, tall, pltpu.VMEM((rows, 7 * N), BF16),
            *(slots,) * 5, *(one,) * 3, *(cross_slots,) * 5, *(cross_one,) * 3,
            pltpu.SemaphoreType.DMA((2, 4)), pltpu.SemaphoreType.DMA((2, 4)), pltpu.SemaphoreType.DMA((2, 4)),
        ],
        compiler_params=pltpu.CompilerParams(collective_id=0, has_side_effects=True, vmem_limit_bytes=53 << 20),
    )(panel, next_panel)
    big = jax.ShapeDtypeStruct((rows, N), F32)
    little = jax.ShapeDtypeStruct((N, N), F32)
    q, r, coupling, trailing = pl.pallas_call(
        functools.partial(finish_kernel, count=count),
        name="finish",
        out_shape=(big, little, little, big),
        in_specs=[vmem, vmem, hbm, hbm],
        out_specs=(hbm, vmem, vmem, hbm),
        scratch_shapes=[
            tall, tall, tall, tall, pltpu.VMEM((rows, 3 * N), BF16), small, small, small, small, small, small, small, small,
            pltpu.SemaphoreType.DMA((2, 8)), pltpu.SemaphoreType.DMA((2, 8)),
        ],
        compiler_params=pltpu.CompilerParams(vmem_limit_bytes=53 << 20),
    )(gram, cross, panel, next_panel)
    return q, r, coupling, trailing


def solution(mesh):
    return jax.shard_map(
        shards,
        mesh=mesh,
        in_specs=(P(("row", "col"), None), P(("row", "col"), None)),
        out_specs=(P(("row", "col"), None), P(), P(), P(("row", "col"), None)),
        check_vma=False,
    )
```

```python
import functools

import jax
import jax.numpy as jnp
from jax import lax
from jax.experimental import pallas as pl
from jax.experimental.pallas import tpu as pltpu
from jax.sharding import PartitionSpec as P

MESH = pl.DeviceIdType.MESH
F32 = jnp.float32
BF16 = jnp.bfloat16
HIGHEST = lax.Precision.HIGHEST
N = 128
T = N // 8
HALF = T // 2
ROW_X = 4
ROW_Y = 8
COL_K = 2
COL_Z = 8
CHUNKS = ROW_X * COL_K
HI, LO, DG, USED, PADDED = 0, 8, 16, 18, 24
CROSS = N // CHUNKS


def two_sum(a, b):
    s = a + b
    t = s - a
    return s, (a - (s - t)) + (b - t)


def quick_sum(a, b):
    s = a + b
    return s, b - (s - a)


def unit(x):
    q = x * (2.0**23 + 1.0)
    return jnp.abs(q - q * (1.0 - 2.0**-24))


def pieces(x, sigma):
    s1 = (x + sigma) - sigma
    x = x - s1
    sigma = sigma * 2.0**-8
    s2 = (x + sigma) - sigma
    x = x - s2
    sigma = sigma * 2.0**-8
    s3 = (x + sigma) - sigma
    return s1.astype(BF16), s2.astype(BF16), s3.astype(BF16), (x - s3).astype(BF16)


def split3(x):
    a = x.astype(BF16)
    x = x - a.astype(F32)
    b = x.astype(BF16)
    return a, b, (x - b.astype(F32)).astype(BF16)


def tdot(a, b):
    return lax.dot_general(a, b, (((0,), (0,)), ((), ())), preferred_element_type=F32)


def dot(a, b, dims=((1,), (0,))):
    return lax.dot_general(a, b, (dims, ((), ())), precision=HIGHEST, preferred_element_type=F32)


def dot3(a, b, dims=((1,), (0,))):
    a1, b1 = a.astype(BF16), b.astype(BF16)
    a2, b2 = (a - a1.astype(F32)).astype(BF16), (b - b1.astype(F32)).astype(BF16)
    left = jnp.concatenate([a1, a1, a2], dims[0][0])
    right = jnp.concatenate([b1, b2, b1], dims[1][0])
    return lax.dot_general(left, right, (dims, ((), ())), preferred_element_type=F32)


def weights(w):
    a, b, c = split3(w)
    ab = jnp.concatenate([a, b], 1)
    return jnp.concatenate([ab, ab], 0), jnp.concatenate([c, a], 0)


def tall_dot(cut, pair):
    a = jnp.dot(cut[:, 0:2 * N], pair[0], preferred_element_type=F32)
    b = jnp.dot(cut[:, N:3 * N], pair[1], preferred_element_type=F32)
    return a[:, :N] + (a[:, N:] + b)


def lane_sub():
    shape = (8, N)
    return lax.broadcasted_iota(jnp.int32, shape, 1), lax.broadcasted_iota(jnp.int32, shape, 0)


def fold(top, low, i):
    lane, sub = lane_sub()
    off = lane - 8 * i
    far = lane - 8 * (T - 1 - i)
    left = pltpu.roll(low, (8 * i + 8) % N, 1)
    block = pltpu.roll(low, (16 * i + 8) % N, 1)
    tile = jnp.where(off > sub, jnp.where(off < 8, block, left), top)
    diag = jnp.sum(jnp.where(far == sub, low, 0.0), axis=0, keepdims=True)
    return tile, diag


def unfold(tile, diag, i):
    lane, sub = lane_sub()
    off = lane - 8 * i
    far = lane - 8 * (T - 1 - i)
    top = jnp.where(off <= sub, tile, 0.0)
    left = pltpu.roll(tile, (N - 8 * i - 8) % N, 1)
    block = pltpu.roll(tile, (N - 16 * i - 8) % N, 1)
    low = jnp.where(far == sub, diag, jnp.where((far > sub) & (far < 8), block, 0.0))
    return top, jnp.where(far < 0, left, low)


def merge(slots, out):
    def pair(h, l, rows):
        hs, ls = slots[0, pl.ds(h, rows)], slots[0, pl.ds(l, rows)]
        for j in range(1, slots.shape[0]):
            hs, e = two_sum(hs, slots[j, pl.ds(h, rows)])
            ls = ls + (slots[j, pl.ds(l, rows)] + e)
        out[pl.ds(h, rows)], out[pl.ds(l, rows)] = quick_sum(hs, ls)

    pair(HI, LO, 8)
    pair(DG, DG + 1, 1)


def plain_merge(slots, out):
    total = slots[0]
    for j in range(1, slots.shape[0]):
        total = total + slots[j]
    out[...] = total


def sums_kernel(
    panel_hbm, next_hbm, gram_ref, cross_ref, panel, nxt, ps,
    gram0, gram1, gram2, gram3, gram4, own1, own2, own3,
    cross0, cross1, cross2, cross3, cross4, part1, part2, part3, in_sem, send_sem, recv_sem,
):
    rows = panel.shape[0]
    step = 1024
    loads = [[] for _ in range(0, rows, step)]
    for j, (src, dst) in enumerate(((panel_hbm, panel), (next_hbm, nxt))):
        for i in range(0, rows, step):
            for h in range(2):
                at = pl.ds(i + h * (step // 2), step // 2)
                loads[i // step].append(pltpu.make_async_copy(src.at[at], dst.at[at], in_sem.at[j, 2 * (i // step) + h]))
                loads[i // step][-1].start()
    r, c = lax.axis_index("row"), lax.axis_index("col")
    y, x = lax.div(r, ROW_X), lax.rem(r, ROW_X)
    z, k = lax.div(c, COL_K), lax.rem(c, COL_K)
    g = x * COL_K + k

    def near(i):
        return (y * ROW_X + lax.div(i, COL_K), z * COL_K + lax.rem(i, COL_K))

    def along_z(i):
        return (r, i * COL_K + k)

    def along_y(i):
        return (i * ROW_X + x, c)

    groups = ((CHUNKS, g, near), (COL_Z, z, along_z), (ROW_Y, y, along_y))
    barrier = pltpu.get_barrier_semaphore()
    for n, me, at in groups:
        for j in range(1, n):
            pl.semaphore_signal(barrier, inc=1, device_id=at(lax.rem(me + j, n)), device_id_type=MESH)

    hi = lo = jnp.zeros((N, N), F32)
    low = jnp.zeros((N, N), F32)
    block = 128
    for i in range(0, rows, step):
        for copy in loads[i // step][:2]:
            copy.wait()
        m = jnp.zeros((8, N), F32)
        for j in range(0, step, block):
            v = jnp.abs(panel[pl.ds(i + j, block), :])
            m = jnp.maximum(m, jnp.max(v.reshape(block // 8, 8, N), axis=0))
        sigma = unit(jnp.max(m, axis=0, keepdims=True)) * (1.5 * 2.0**17)
        for j in range(0, step, block):
            at = pl.ds(i + j, block)
            for n, s in enumerate(pieces(panel[at, :], sigma)):
                ps[at, pl.ds(n * N, N)] = s
        at = pl.ds(i, step)
        e = tdot(ps[at, 0:2 * N], ps[at, 0:4 * N])
        hi, err = two_sum(hi, e[:N, :N])
        lo = lo + err
        hi, err = two_sum(hi, e[:N, N:2 * N] + e[N:, :N])
        lo = lo + err + e[N:, N:2 * N]
        low = low + ((e[:N, 2 * N:3 * N] + e[:N, 3 * N:4 * N]) + (e[N:, 2 * N:3 * N] + e[N:, 3 * N:4 * N]))
    lo = lo + (low + low.T)
    hi, lo = quick_sum(hi, lo)
    for i in range(CHUNKS):
        a, b = slice(8 * i, 8 * i + 8), slice(8 * (T - 1 - i), 8 * (T - i))
        ht, hd = fold(hi[a], hi[b], i)
        lt, ld = fold(lo[a], lo[b], i)
        gram0[i, pl.ds(HI, 8)] = ht
        gram0[i, pl.ds(LO, 8)] = lt
        gram0[i, pl.ds(DG, 1)] = hd
        gram0[i, pl.ds(DG + 1, 1)] = ld

    pl.semaphore_wait(barrier, sum(n - 1 for n, _, _ in groups))

    def spread(stream, phase, group, source, target, used):
        n, me, at = group
        for j in sorted(range(1, n), key=lambda j: abs(2 * j - n)):
            to = lax.rem(me + j, n)
            pltpu.make_async_remote_copy(
                source(to).at[pl.ds(0, used)], target(j).at[pl.ds(0, used)],
                send_sem.at[stream, phase], recv_sem.at[stream, phase], device_id=at(to), device_id_type=MESH,
            ).start()

    def arrived(sem, stream, phase, n):
        whole = (gram0.at[pl.ds(0, n - 1), pl.ds(0, USED)], cross0.at[pl.ds(0, n - 1)])[stream]
        pltpu.make_async_copy(whole, whole, sem.at[stream, phase]).wait()

    class Stream:
        def __init__(self, stream, first, slots, own, add, used):
            self.stream, self.first, self.slots, self.own, self.add, self.used = stream, first, slots, own, add, used

        def scatter(self):
            spread(self.stream, 0, groups[0], lambda to: self.first.at[to], lambda j: self.slots[0].at[CHUNKS - j], self.used)
            self.slots[0][0] = self.first[g]

        def forward(self, phase):
            group = groups[(phase + 1) % 3]
            slot = group[1]
            arrived(recv_sem, self.stream, phase, groups[phase][0])
            own = self.own[phase]
            self.add(self.slots[phase], own)
            spread(self.stream, phase + 1, group, lambda to: own, lambda j: self.slots[phase + 1].at[slot], self.used)
            self.slots[phase + 1][slot] = own[...]

    gram = Stream(0, gram0, (gram1, gram2, gram3, gram4), (own1, own2, own3), merge, USED)
    cross = Stream(1, cross0, (cross1, cross2, cross3, cross4), (part1, part2, part3), plain_merge, CROSS)
    gram.scatter()
    total = jnp.zeros((N, N), F32)
    for i in range(0, rows, step):
        for copy in loads[i // step][2:]:
            copy.wait()
        for j in range(0, step, block):
            at = pl.ds(i + j, block)
            for n, s in enumerate(split3(nxt[at, :])):
                ps[at, pl.ds((4 + n) * N, N)] = s
        at = pl.ds(i, step)
        e = tdot(ps[at, 0:2 * N], ps[at, 4 * N:7 * N])
        w = tdot(ps[at, 2 * N:4 * N], ps[at, 4 * N:6 * N])
        part = (e[:N, 2 * N:] + e[N:, 2 * N:]) + ((w[:N, :N] + w[:N, N:]) + w[N:, :N])
        part = part + ((e[:N, N:2 * N] + e[N:, :N]) + e[N:, N:2 * N])
        total = total + (e[:N, :N] + part)
    for i in range(CHUNKS):
        cross0[i] = total[CROSS * i:CROSS * (i + 1)]
    cross.scatter()
    for phase in range(3):
        gram.forward(phase)
        cross.forward(phase)
    arrived(recv_sem, 0, 3, CHUNKS)
    gram_ref[...] = gram4[...]
    arrived(recv_sem, 1, 3, CHUNKS)
    cross_ref[...] = cross4[...]
    for stream in range(2):
        for phase, n in enumerate((CHUNKS, COL_Z, ROW_Y, CHUNKS)):
            arrived(send_sem, stream, phase, n)


def lanes(v, i):
    return jnp.broadcast_to(v[:, i:i + 1], (8, N))


def subs(v, i):
    return jnp.broadcast_to(v[i:i + 1, :], (8, N))


def factor(gram, upper, lower_inv):
    lane, sub = lane_sub()
    a = [gram[8 * b:8 * b + 8, :] for b in range(T)]
    t = [lanes(a[0], i) for i in range(8)]
    for b in range(T):
        off = lane - 8 * b
        inside = (off >= 0) & (off < 8)
        d = {(i, j): subs(t[j], i) for i in range(8) for j in range(i, 8)}
        rs, h = [], {}
        for i in range(8):
            rs.append(lax.rsqrt(d[i, i]))
            for j in range(i + 1, 8):
                h[i, j] = rs[i] * d[i, j]
            for k in range(i + 1, 8):
                for j in range(k, 8):
                    d[k, j] = d[k, j] - h[i, k] * h[i, j]
        ahead = f2 = None
        if b + 1 < T:
            ahead = [lanes(a[b + 1], 8 * (b + 1) + j) for j in range(8)]
            f2 = [lanes(a[b + 1], 8 * b + i) for i in range(8)]
            for i in range(8):
                f2[i] = f2[i] * rs[i]
                for j in range(i + 1, 8):
                    f2[j] = f2[j] - f2[i] * h[i, j]
                for j in range(8):
                    ahead[j] = ahead[j] - f2[i] * subs(f2[i], j)
        v = jnp.where(inside, jnp.where(off == sub, 1.0, 0.0), a[b])
        g = []
        scale = rs[0]
        for i in range(8):
            if i:
                scale = jnp.where(sub == i, rs[i], scale)
            g.append(rs[i] * subs(v, i))
            if i < 7:
                below = jnp.where(sub > i, t[i] * rs[i], 0.0)
                v = v - below * g[i]
                for j in range(i + 1, 8):
                    t[j] = t[j] - below * h[i, j]
        lower_inv[8 * b:8 * b + 8, :] = jnp.where(off < 8, v * scale, 0.0)
        u = v
        for j in range(8):
            u = jnp.where(off == j, jnp.where(sub <= j, t[j], 0.0), u)
        upper[8 * b:8 * b + 8, :] = jnp.where(off < 0, 0.0, u * scale)
        for b2 in range(b + 1, T):
            if b2 > b + 1:
                f2 = [lanes(a[b2], 8 * b + i) for i in range(8)]
            v2 = jnp.where(inside, 0.0, a[b2])
            for i in range(8):
                if b2 > b + 1:
                    f2[i] = f2[i] * rs[i]
                    for j in range(i + 1, 8):
                        f2[j] = f2[j] - f2[i] * h[i, j]
                v2 = v2 - f2[i] * g[i]
            a[b2] = v2
        t = ahead


def finish_kernel(
    sums, cross_sum, panel_hbm, next_hbm, q_hbm, r_ref, coupling_ref, trailing_hbm,
    panel, nxt, q, trail, cut, hi_ref, lo_ref, gram, r1, x1, gram2, r2, x2, in_sem, out_sem, *, count,
):
    rows = panel.shape[0]
    block = 256
    loads = [
        pltpu.make_async_copy(panel_hbm, panel, in_sem.at[0, 0]),
        pltpu.make_async_copy(next_hbm, nxt, in_sem.at[1, 0]),
    ]
    for copy in loads:
        copy.start()
    for i in range(HALF):
        a, b = slice(8 * i, 8 * i + 8), slice(8 * (T - 1 - i), 8 * (T - i))
        for ref, at, dg in ((hi_ref, HI, DG), (lo_ref, LO, DG + 1)):
            ref[a, :], ref[b, :] = unfold(sums[i, pl.ds(at, 8)], sums[i, pl.ds(dg, 1)], i)
    row_id = lax.broadcasted_iota(jnp.int32, (N, N), 0)
    col_id = lax.broadcasted_iota(jnp.int32, (N, N), 1)
    eye = row_id == col_id

    def whole(ref):
        half = ref[...]
        return jnp.where(eye, half, half + half.T) * (1.0 / count)

    hi, lo = whole(hi_ref), whole(lo_ref)
    diag = jnp.where(eye, hi, 0.0)
    s_row = unit(lax.rsqrt(jnp.sum(diag, axis=0, keepdims=True)))
    s_col = unit(lax.rsqrt(jnp.sum(diag, axis=1, keepdims=True)))
    hi = hi * s_row * s_col
    lo = lo * s_row * s_col
    gram[...] = hi
    factor(gram, r1, x1)
    s1, s2, s3, s4 = pieces(r1[...], 1.5 * 2.0**15)
    p12, p34 = jnp.concatenate([s1, s2], 1), jnp.concatenate([s3, s4], 1)
    e = tdot(p12, jnp.concatenate([p12, p34], 1))
    low = (e[:N, 2 * N:3 * N] + e[:N, 3 * N:]) + (e[N:, 2 * N:3 * N] + e[N:, 3 * N:])
    low = (low + low.T) + e[N:, N:2 * N]
    rest, e1 = two_sum(hi, -e[:N, :N])
    rest, e2 = two_sum(rest, -(e[:N, N:2 * N] + e[N:, :N]))
    rest = rest + ((e1 + e2) + (lo - low))
    x = x1[...]
    m = dot(x, r1[...], ((1,), (1,)))
    y = dot3(x, rest)
    gram2[...] = dot(m, m, ((1,), (1,))) + dot3(y, x, ((1,), (1,)))
    cross = dot(x, cross_sum[...].reshape(N, N) * (1.0 / count) * s_col)
    pair = weights((x * s_row).T)
    for copy in loads:
        copy.wait()

    def pieces_of(v):
        first, second, third = split3(v)
        return jnp.concatenate([second, first, third], 1)

    for i in range(0, rows, block):
        at = pl.ds(i, block)
        cut[at, :] = pieces_of(tall_dot(pieces_of(panel[at, :]), pair))
    factor(gram2, r2, x2)
    coupling = dot(x2[...], cross)
    coupling_ref[...] = coupling
    pair = weights(x2[...].T)
    copies = []

    def send(src, dst, j, i):
        at = pl.ds(i, block)
        copies.append(pltpu.make_async_copy(src.at[at], dst.at[at], out_sem.at[j, i // block]))
        copies[-1].start()

    for i in range(0, rows, block):
        at = pl.ds(i, block)
        q[at, :] = tall_dot(cut[at, :], pair)
        send(q, q_hbm, 0, i)
    back = weights(dot(x2[...], coupling, ((0,), (0,))))
    for i in range(0, rows, block):
        at = pl.ds(i, block)
        trail[at, :] = nxt[at, :] - tall_dot(cut[at, :], back)
        send(trail, trailing_hbm, 1, i)
    r_ref[...] = dot(r2[...], r1[...]) / s_row
    for copy in copies:
        copy.wait()


def shards(panel, next_panel):
    rows = panel.shape[0]
    count = rows * lax.axis_size("row") * lax.axis_size("col")
    hbm, vmem = pl.BlockSpec(memory_space=pltpu.HBM), pl.BlockSpec(memory_space=pltpu.VMEM)
    small = pltpu.VMEM((N, N), F32)
    tall = pltpu.VMEM((rows, N), F32)
    slots = pltpu.VMEM((CHUNKS, PADDED, N), F32)
    one = pltpu.VMEM((PADDED, N), F32)
    cross_slots = pltpu.VMEM((CHUNKS, CROSS, N), F32)
    cross_one = pltpu.VMEM((CROSS, N), F32)
    gram, cross = pl.pallas_call(
        sums_kernel,
        name="sums",
        out_shape=(jax.ShapeDtypeStruct((CHUNKS, PADDED, N), F32), jax.ShapeDtypeStruct((CHUNKS, CROSS, N), F32)),
        in_specs=[hbm, hbm],
        out_specs=(vmem, vmem),
        scratch_shapes=[
            tall, tall, pltpu.VMEM((rows, 7 * N), BF16),
            *(slots,) * 5, *(one,) * 3, *(cross_slots,) * 5, *(cross_one,) * 3,
            pltpu.SemaphoreType.DMA((2, 4)), pltpu.SemaphoreType.DMA((2, 4)), pltpu.SemaphoreType.DMA((2, 4)),
        ],
        compiler_params=pltpu.CompilerParams(collective_id=0, has_side_effects=True, vmem_limit_bytes=53 << 20),
    )(panel, next_panel)
    big = jax.ShapeDtypeStruct((rows, N), F32)
    little = jax.ShapeDtypeStruct((N, N), F32)
    q, r, coupling, trailing = pl.pallas_call(
        functools.partial(finish_kernel, count=count),
        name="finish",
        out_shape=(big, little, little, big),
        in_specs=[vmem, vmem, hbm, hbm],
        out_specs=(hbm, vmem, vmem, hbm),
        scratch_shapes=[
            tall, tall, tall, tall, pltpu.VMEM((rows, 3 * N), BF16), small, small, small, small, small, small, small, small,
            pltpu.SemaphoreType.DMA((2, 8)), pltpu.SemaphoreType.DMA((2, 8)),
        ],
        compiler_params=pltpu.CompilerParams(vmem_limit_bytes=53 << 20),
    )(gram, cross, panel, next_panel)
    return q, r, coupling, trailing


def solution(mesh):
    return jax.shard_map(
        shards,
        mesh=mesh,
        in_specs=(P(("row", "col"), None), P(("row", "col"), None)),
        out_specs=(P(("row", "col"), None), P(), P(), P(("row", "col"), None)),
        check_vma=False,
    )
```
